32 devices in a mesh: inner: 4 (over z), outer: 8 (over y, x, core).
Axes of the slice: x: 2, y: 2, z: 4, core: 2. Of those that a mesh axis runs over, the one named last changes fastest.
Arguments:
- features: bfloat16 [262144, 256], P(('inner', 'outer')), may hold values from -6 to 6
- tiles: bfloat16 [2048, 8, 128, 128], P(('inner', 'outer')), may hold values from -0.1875 to 0.1875
- tile_src: int32 [2048, 8], P(('inner', 'outer')), may hold values from 0 to 111, as said below
- tile_count: int32 [2048], P(('inner', 'outer')), may hold values from 1 to 8
- node_count: int32 [32], P(('inner', 'outer')), may hold values from 2730 to 8192
- boundary: int32 [32, 8], P(('inner', 'outer')), may hold values from 0 to 63, as said below
- send_inner: int32 [32, 4, 4], P(('inner', 'outer')), may hold values from 0 to 7
- count_inner: int32 [32, 4], P(('inner', 'outer')), may hold values from 0 to 4, as said below
- send_outer: int32 [32, 8, 4], P(('inner', 'outer')), may hold values from 0 to 7
- count_outer: int32 [32, 8], P(('inner', 'outer')), may hold values from 0 to 4, as said below
- w_first: bfloat16 [256, 256], replicated, may hold values from -0.375 to 0.375
- gamma: float32 [256], replicated, may hold values from 0.25 to 1.75
- beta: float32 [256], replicated, may hold values from -3 to 3
- w_second: bfloat16 [256, 256], replicated, may hold values from -0.375 to 0.375
- b_second: float32 [256], replicated, may hold values from -3 to 3
Outputs:
- updated: bfloat16 [262144, 256], P(('inner', 'outer'))
The draws below stay inside these ranges and needn't reach their ends.
Inputs may be any that keep to these rules, and one draw needn't show every extreme that they name: `tile_src`: index into the partition's source table; a slot index that is read names a slot its sender fills. `boundary`: distinct block numbers within a partition. `count_inner`: zero toward the partition itself, at least one toward every other peer. `count_outer`: zero toward the partition itself, at least one toward every other peer.
All inputs are finite; a program needn't handle non-finite values.
Results may differ from the reference program's by a relative error of at most 0.0053.
Values may be sent and summed in bfloat16 or wider, within the bound.
A program may use at most 128 MiB of HBM per device.

```python
import jax
import jax.numpy as jnp
from jax import lax

F = 256
H = 256
R = 128
NB = 64
TPB = 8
BND = 8
CAP = 4
NODE_DEV = 8192
NODES = 262144
NSRC = 112
N_INNER = 4
N_OUTER = 8
DEVICES = 32


def send_counts(key):
    base = jax.random.fold_in(key, 11)
    target = jax.random.randint(jax.random.fold_in(base, 1), (), 0, DEVICES)
    target = jnp.where(target % N_OUTER == N_OUTER - 1, target - 1, target)
    device = jnp.arange(DEVICES)[:, None]
    inner_peer = jnp.arange(N_INNER)[None, :]
    inner_recv = inner_peer * N_OUTER + device % N_OUTER
    inner_cnt = jax.random.randint(jax.random.fold_in(base, 2), (DEVICES, N_INNER), 1, CAP + 1)
    inner_cnt = jnp.where(inner_recv == target, CAP, inner_cnt)
    inner_cnt = jnp.where(inner_recv == device, 0, inner_cnt)
    outer_peer = jnp.arange(N_OUTER)[None, :]
    outer_recv = device // N_OUTER * N_OUTER + outer_peer
    outer_cnt = jax.random.randint(jax.random.fold_in(base, 3), (DEVICES, N_OUTER), 1, CAP + 1)
    outer_cnt = jnp.where(outer_recv == target, CAP, outer_cnt)
    outer_cnt = jnp.where(outer_recv == device, 0, outer_cnt)
    return (inner_cnt.astype(jnp.int32), outer_cnt.astype(jnp.int32), target)


def draw_count_inner(key, part):
    return send_counts(key)[0]


def draw_count_outer(key, part):
    return send_counts(key)[1]


def draw_tile_src(key, part):
    inner_cnt, outer_cnt, target = send_counts(key)
    rows_all = DEVICES * NB
    raw = jax.random.randint(jax.random.fold_in(key, 21), (rows_all, TPB), 0, NSRC)
    device = (jnp.arange(rows_all) // NB)[:, None]
    spot = raw - NB
    inner_peer = jnp.clip(spot // CAP, 0, N_INNER - 1)
    inner_slot = spot % CAP
    inner_sender = inner_peer * N_OUTER + device % N_OUTER
    inner_ok = (spot >= 0) & (spot < N_INNER * CAP) & (inner_slot < inner_cnt[inner_sender, device // N_OUTER])
    rest = spot - N_INNER * CAP
    outer_peer = jnp.clip(rest // CAP, 0, N_OUTER - 1)
    outer_slot = rest % CAP
    outer_sender = device // N_OUTER * N_OUTER + outer_peer
    outer_ok = (rest >= 0) & (outer_slot < outer_cnt[outer_sender, device % N_OUTER])
    result = jnp.where((raw < NB) | inner_ok | outer_ok, raw, raw % NB)
    result = result.at[target * NB, 0].set(NSRC - 1)
    result = result.at[target * NB, 1].set(0)
    return result.astype(jnp.int32)


def draw_tile_count(key, part):
    counts = jax.random.randint(jax.random.fold_in(key, 31), (DEVICES * NB,), 1, TPB + 1)
    chosen = jax.random.randint(jax.random.fold_in(key, 32), (), 0, DEVICES * NB)
    return counts.at[chosen].set(TPB).astype(jnp.int32)


def draw_node_count(key, part):
    device = jnp.arange(DEVICES)
    lowest = NODE_DEV // 3
    rising = lowest + (NODE_DEV - lowest) * device // max(DEVICES - 1, 1)
    jitter = jax.random.randint(jax.random.fold_in(key, 41), (DEVICES,), 0, R)
    jitter = jnp.where((device == 0) | (device == DEVICES - 1), 0, jitter)
    return jnp.maximum(rising - jitter, lowest).astype(jnp.int32)


def draw_boundary(key, part):
    keys = jax.random.split(jax.random.fold_in(key, 51), DEVICES)

    def pick_blocks(single):
        return jax.random.permutation(single, NB)[:BND]
    return jax.vmap(pick_blocks)(keys).astype(jnp.int32)


def set_ends(entries, rng, smallest, largest):
    longest = entries.shape.index(max(entries.shape))
    spots = []
    for shift in (0, 1):
        where = [jax.random.randint(jax.random.fold_in(rng, axis), (), 0, length) for axis, length in enumerate(entries.shape)]
        where[longest] = (where[longest] + shift) % entries.shape[longest]
        spots.append(tuple(where))
    return entries.at[spots[0]].set(smallest).at[spots[1]].set(largest)


def block_scale(own_key, dims, shards, smallest, largest):
    def one(axis_at, shards_of):
        steps = jax.random.uniform(jax.random.fold_in(jax.random.fold_in(own_key, 6), axis_at), (shards_of,), jnp.float32, smallest / len(shards), largest / len(shards))
        return jnp.repeat(jnp.exp(steps), dims[axis_at] // shards_of).reshape((-1,) + (1,) * (len(dims) - axis_at - 1))

    loudness = one(*shards[0])
    for cut in shards[1:]:
        loudness = loudness * one(*cut)
    return loudness


def normal_values(key, dims, spread, most, cuts=(), kind=jnp.bfloat16):
    values = spread * jax.random.normal(key, dims, jnp.float32)
    if cuts:
        values = values * block_scale(key, dims, cuts, -0.22, 0.18)
    return jnp.clip(values, -most, most).astype(kind)


def setup_inputs(seed: int = 0) -> dict:
    splits = jax.random.split(jax.random.key(seed), 16)
    features = normal_values(splits[0], (NODES, F), 1.0, 6.0, ((0, 32),))
    tiles = normal_values(splits[1], (DEVICES * NB, TPB, R, R), (R * TPB) ** -0.5, 0.1875, ((0, 32),))
    tile_src = draw_tile_src(jax.random.fold_in(splits[15], 71), 0)
    tile_count = draw_tile_count(jax.random.fold_in(splits[15], 71), 0)
    node_count = draw_node_count(jax.random.fold_in(splits[15], 71), 0)
    boundary = draw_boundary(jax.random.fold_in(splits[15], 71), 0)
    send_inner = set_ends(jax.random.randint(splits[6], (DEVICES, N_INNER, CAP), 0, BND), jax.random.fold_in(splits[6], 1), 0, BND - 1).astype(jnp.int32)
    count_inner = draw_count_inner(jax.random.fold_in(splits[15], 71), 0)
    send_outer = set_ends(jax.random.randint(splits[8], (DEVICES, N_OUTER, CAP), 0, BND), jax.random.fold_in(splits[8], 1), 0, BND - 1).astype(jnp.int32)
    count_outer = draw_count_outer(jax.random.fold_in(splits[15], 71), 0)
    w_first = normal_values(splits[10], (F, H), F ** -0.5, 0.375)
    gamma = jnp.clip(1.0 + 0.15 * jax.random.normal(splits[11], (H,), jnp.float32), 0.25, 1.75)
    beta = normal_values(splits[12], (H,), 0.5, 3.0, (), jnp.float32)
    w_second = normal_values(splits[13], (H, F), H ** -0.5, 0.375)
    b_second = normal_values(splits[14], (F,), 0.5, 3.0, (), jnp.float32)
    return dict(features=features, tiles=tiles, tile_src=tile_src, tile_count=tile_count, node_count=node_count, boundary=boundary, send_inner=send_inner, count_inner=count_inner, send_outer=send_outer, count_outer=count_outer, w_first=w_first, gamma=gamma, beta=beta, w_second=w_second, b_second=b_second)


EPSILON = 1e-05

def reference(features, tiles, tile_src, tile_count, node_count, boundary, send_inner, count_inner, send_outer, count_outer, w_first, gamma, beta, w_second, b_second):
    zero_bf = jnp.zeros((), jnp.bfloat16)
    row_index = jnp.arange(NB * R).reshape(1, NB, R)
    live = row_index < node_count.reshape(DEVICES, 1, 1)
    blocked = jnp.where(live[..., None], features.reshape(DEVICES, NB, R, F), zero_bf)
    tile_all = tiles.reshape(DEVICES, NB, TPB, R, R)
    source_all = tile_src.reshape(DEVICES, NB, TPB)
    used_all = jnp.arange(TPB).reshape(1, 1, TPB) < tile_count.reshape(DEVICES, NB, 1)
    slots = jnp.arange(CAP).reshape(1, CAP)

    def incoming(senders, lists, counts):
        chosen = boundary[senders[:, None], lists]
        pieces = blocked[senders[:, None], chosen]
        keep = slots < counts[:, None]
        return jnp.where(keep[:, :, None, None], pieces, zero_bf).reshape(-1, R, F)

    def hidden_first(device):
        outer_pos = device % N_OUTER
        inner_pos = device // N_OUTER
        inner_senders = jnp.arange(N_INNER) * N_OUTER + outer_pos
        outer_senders = inner_pos * N_OUTER + jnp.arange(N_OUTER)
        from_inner = incoming(inner_senders, send_inner[inner_senders, inner_pos], count_inner[inner_senders, inner_pos])
        from_outer = incoming(outer_senders, send_outer[outer_senders, outer_pos], count_outer[outer_senders, outer_pos])
        local = blocked[device]
        table = jnp.concatenate([local, from_inner, from_outer], axis=0)
        gathered = table[source_all[device]].astype(jnp.float32)
        weights = jnp.where(used_all[device][:, :, None, None], tile_all[device], zero_bf).astype(jnp.float32)
        summed = jnp.einsum('bjrk,bjkf->brf', weights, gathered)
        combined = (local.astype(jnp.float32) + summed).astype(jnp.bfloat16).reshape(NB * R, F)
        return jnp.dot(combined, w_first, preferred_element_type=jnp.float32)
    first = lax.map(hidden_first, jnp.arange(DEVICES))
    mask = live.reshape(DEVICES, NB * R, 1)
    total = jnp.sum(node_count).astype(jnp.float32)
    mean = lax.optimization_barrier(jnp.sum(jnp.where(mask, first, 0.0), axis=(0, 1))) / total
    variance = lax.optimization_barrier(jnp.sum(jnp.where(mask, jnp.square(first - mean), 0.0), axis=(0, 1))) / total
    normed = jax.nn.relu(gamma.astype(jnp.float32) * (first - mean) * lax.rsqrt(variance + EPSILON) + beta.astype(jnp.float32)).astype(jnp.bfloat16)
    output = jnp.dot(normed.reshape(-1, H), w_second, preferred_element_type=jnp.float32) + b_second.astype(jnp.float32)
    output = jnp.where(mask.reshape(-1, 1), output, 0.0).astype(jnp.bfloat16)
    return output
```

```python
import functools

import jax
import jax.numpy as jnp
from jax import lax
from jax.experimental import pallas as pl
from jax.experimental.pallas import tpu as pltpu
from jax.sharding import PartitionSpec as P

EPSILON = 1e-05
MESH = pl.DeviceIdType.MESH
BF16 = jnp.bfloat16
F32 = jnp.float32
DEPTH = 4
GROUP = 4


def peers_of(n_inner, n_outer):
    i, o = lax.axis_index("inner"), lax.axis_index("outer")
    inner = [((lax.rem(i + k, n_inner), o), k) for k in range(1, n_inner)]
    outer = [((i, lax.rem(o + k, n_outer)), k) for k in range(1, n_outer)]
    return inner, outer


def enter(partners):
    barrier = pltpu.get_barrier_semaphore()
    for device, _ in partners:
        pl.semaphore_signal(barrier, inc=1, device_id=device, device_id_type=MESH)
    pl.semaphore_wait(barrier, len(partners))


def exchange_kernel(
    n_inner,
    n_outer,
    src_ref,
    count_ref,
    node_ref,
    border_ref,
    send_in_ref,
    send_out_ref,
    feat_ref,
    tile_ref,
    recv_ref,
    part_ref,
    table,
    packed,
    tile_buf,
    part_buf,
    feat_sem,
    zero_sem,
    tile_sem,
    part_sem,
    send_sem,
    recv_sem,
):
    nb, per_block, rows = tile_ref.shape[0], tile_ref.shape[1], tile_ref.shape[2]
    width = feat_ref.shape[2]
    cap = send_in_ref.shape[2]
    i, o = lax.axis_index("inner"), lax.axis_index("outer")
    inner, outer = peers_of(n_inner, n_outer)
    filled = node_ref[0]
    row_ids = lax.broadcasted_iota(jnp.int32, (rows, width), 0)

    feats = pltpu.make_async_copy(feat_ref, table.at[pl.ds(0, nb)], feat_sem)
    feats.start()

    def tile_copy(b, slot):
        return pltpu.make_async_copy(tile_ref.at[b], tile_buf.at[slot], tile_sem.at[slot])

    def part_copy(b, slot):
        return pltpu.make_async_copy(part_buf.at[slot], part_ref.at[b], part_sem.at[slot])

    for d in range(DEPTH):
        tile_copy(d, d).start()
    enter(inner + outer)
    feats.wait()
    table[nb] = jnp.zeros((rows, width), BF16)

    def live_block(block):
        data = table[block].astype(F32)
        return jnp.where(row_ids < filled - block * rows, data, 0.0).astype(BF16)

    copies = []
    order = []
    for k in range(max(n_inner, n_outer)):
        if k < len(inner):
            order.append((inner[k], True))
        if k < len(outer):
            order.append((outer[k], False))
    for at, ((device, step), is_inner) in enumerate(order):
        for c in range(cap):
            if is_inner:
                entry = send_in_ref[0, device[0], c]
            else:
                entry = send_out_ref[0, device[1], c]
            packed[at, c] = live_block(border_ref[0, entry])
        first_slot = i * cap if is_inner else (n_inner + o) * cap
        copy = pltpu.make_async_remote_copy(
            src_ref=packed.at[at],
            dst_ref=recv_ref.at[pl.ds(first_slot, cap)],
            send_sem=send_sem.at[at],
            recv_sem=recv_sem.at[at],
            device_id=device,
            device_id_type=MESH,
        )
        copy.start()
        copies.append(copy)

    @pl.loop(0, nb)
    def _(block):
        table[block] = live_block(block)

    last = recv_ref.shape[0] - 1
    zeros = pltpu.make_async_copy(table.at[nb], recv_ref.at[last], zero_sem)
    zeros.start()

    def one(b, slot, wait_part, more):
        tile_copy(b, slot).wait()
        used = count_ref[b]
        total = table[b].astype(F32)
        for pair in range(per_block // 2):
            weights, sources = [], []
            for j in (2 * pair, 2 * pair + 1):
                s = src_ref[b, j]
                ok = jnp.logical_and(s < nb, j < used)
                sources.append(table[jnp.where(ok, s, nb)])
                weights.append(tile_buf[slot, j])
            total += jnp.dot(
                jnp.concatenate(weights, axis=1),
                jnp.concatenate(sources, axis=0),
                preferred_element_type=F32,
            )
        if wait_part:
            part_copy(b - DEPTH, slot).wait()
        part_buf[slot] = total
        part_copy(b, slot).start()
        if more:
            tile_copy(b + DEPTH, slot).start()

    for d in range(DEPTH):
        one(d, d, False, True)

    @pl.loop(1, nb // DEPTH - 1)
    def _(g):
        for d in range(DEPTH):
            one(g * DEPTH + d, d, True, True)

    for d in range(DEPTH):
        one(nb - DEPTH + d, d, True, False)
    for d in range(DEPTH):
        part_copy(nb - DEPTH + d, d).wait()
    zeros.wait()
    for copy in copies:
        copy.wait()


def exchange(mesh_sizes, tile_src, tile_count, node_count, boundary, send_inner, send_outer, blocks, tiles):
    n_inner, n_outer = mesh_sizes
    nb, per_block, rows = tiles.shape[:3]
    width = blocks.shape[2]
    cap = send_inner.shape[2]
    slots = (n_inner + n_outer) * cap + 1
    partners = n_inner + n_outer - 2
    smem = pl.BlockSpec(memory_space=pltpu.SMEM)
    hbm = pl.BlockSpec(memory_space=pl.ANY)
    return pl.pallas_call(
        functools.partial(exchange_kernel, n_inner, n_outer),
        out_shape=(
            jax.ShapeDtypeStruct((slots, rows, width), BF16),
            jax.ShapeDtypeStruct((nb, rows, width), F32),
        ),
        in_specs=[smem] * 6 + [hbm] * 2,
        out_specs=(hbm, hbm),
        scratch_shapes=[
            pltpu.VMEM((nb + 1, rows, width), BF16),
            pltpu.VMEM((partners, cap, rows, width), BF16),
            pltpu.VMEM((DEPTH, per_block, rows, rows), BF16),
            pltpu.VMEM((DEPTH, rows, width), F32),
            pltpu.SemaphoreType.DMA,
            pltpu.SemaphoreType.DMA,
            pltpu.SemaphoreType.DMA((DEPTH,)),
            pltpu.SemaphoreType.DMA((DEPTH,)),
            pltpu.SemaphoreType.DMA((partners,)),
            pltpu.SemaphoreType.DMA((partners,)),
        ],
        compiler_params=pltpu.CompilerParams(
            collective_id=0, has_side_effects=True, vmem_limit_bytes=40 << 20
        ),
    )(tile_src, tile_count, node_count, boundary, send_inner, send_outer, blocks, tiles)


def remote_kernel(
    src_ref, count_ref, node_ref, recv_ref, tile_ref, part_ref, w_ref, out_ref, stats_ref
):
    step = pl.program_id(0)
    nb_all = src_ref.shape[0]
    group, per_block, rows = tile_ref.shape[:3]
    width = part_ref.shape[2]
    zero_slot = recv_ref.shape[0] - 1
    filled = node_ref[0]

    @pl.when(step == 0)
    def _():
        stats_ref[...] = jnp.zeros_like(stats_ref)

    found = []
    for g in range(group):
        b = step * group + g
        used = count_ref[b]
        code, n = jnp.int32(0), jnp.int32(0)
        for j in range(per_block):
            hit = jnp.logical_and(src_ref[b, j] >= nb_all, j < used).astype(jnp.int32)
            code = code + hit * jnp.left_shift(jnp.int32(j), 3 * n)
            n = n + hit
        found.append((b, code, n))

    def pair_product(g, pair):
        b, code, n = found[g]
        weights, sources = [], []
        for rank in (2 * pair, 2 * pair + 1):
            j = jnp.bitwise_and(jnp.right_shift(code, 3 * rank), 7)
            slot = jnp.where(rank < n, src_ref[b, j] - nb_all, zero_slot)
            sources.append(recv_ref[slot])
            weights.append(tile_ref[g, j])
        return jnp.dot(
            jnp.concatenate(weights, axis=1),
            jnp.concatenate(sources, axis=0),
            preferred_element_type=F32,
        )

    for g in range(group):
        part_ref[g] += pair_product(g, 0)
    for g in range(group):
        for pair in range(1, per_block // 2):

            @pl.when(found[g][2] > 2 * pair)
            def _():
                part_ref[g] += pair_product(g, pair)

    combined = part_ref[...].reshape(group * rows, width).astype(BF16)
    out_ref[...] = combined
    first = jnp.dot(combined, w_ref[...], preferred_element_type=F32)
    row_ids = lax.broadcasted_iota(jnp.int32, first.shape, 0)
    kept = jnp.where(row_ids < filled - step * group * rows, first, 0.0)
    stats_ref[0:1, :] += jnp.sum(kept, axis=0, keepdims=True)
    stats_ref[1:2, :] += jnp.sum(kept * kept, axis=0, keepdims=True)

    @pl.when(step == 0)
    def _():
        stats_ref[2:3, :] = jnp.full((1, stats_ref.shape[1]), filled.astype(F32))


def remote_tiles(tile_src, tile_count, node_count, recv, tiles, part, w_first):
    nb, per_block, rows = tiles.shape[:3]
    width = part.shape[2]
    hidden = w_first.shape[1]
    return pl.pallas_call(
        remote_kernel,
        grid_spec=pltpu.PrefetchScalarGridSpec(
            num_scalar_prefetch=3,
            grid=(nb // GROUP,),
            in_specs=[
                pl.BlockSpec(recv.shape, lambda s, *_: (0, 0, 0)),
                pl.BlockSpec((GROUP, per_block, rows, rows), lambda s, *_: (s, 0, 0, 0)),
                pl.BlockSpec((GROUP, rows, width), lambda s, *_: (s, 0, 0)),
                pl.BlockSpec(w_first.shape, lambda s, *_: (0, 0)),
            ],
            out_specs=[
                pl.BlockSpec((GROUP * rows, width), lambda s, *_: (s, 0)),
                pl.BlockSpec((8, hidden), lambda s, *_: (0, 0)),
            ],
        ),
        out_shape=(
            jax.ShapeDtypeStruct((nb * rows, width), BF16),
            jax.ShapeDtypeStruct((8, hidden), F32),
        ),
        compiler_params=pltpu.CompilerParams(vmem_limit_bytes=40 << 20),
    )(tile_src, tile_count, node_count, recv, tiles, part, w_first)


def totals_kernel(n_inner, n_outer, stats_ref, out_ref, first_buf, second_buf, mid, send_sem, recv_sem):
    i, o = lax.axis_index("inner"), lax.axis_index("outer")
    inner, outer = peers_of(n_inner, n_outer)
    enter(inner + outer)

    def round_of(partners, source, buf, me, base):
        copies = []
        for at, (device, _) in enumerate(partners):
            copy = pltpu.make_async_remote_copy(
                src_ref=source,
                dst_ref=buf.at[me],
                send_sem=send_sem.at[base + at],
                recv_sem=recv_sem.at[base + at],
                device_id=device,
                device_id_type=MESH,
            )
            copy.start()
            copies.append(copy)
        buf[me] = source[...]
        for copy in copies:
            copy.wait()
        return jnp.sum(buf[...], axis=0)

    mid[...] = round_of(outer, stats_ref, first_buf, o, 0)
    out_ref[...] = round_of(inner, mid, second_buf, i, len(outer))


def all_totals(mesh_sizes, stats):
    n_inner, n_outer = mesh_sizes
    partners = n_inner + n_outer - 2
    vmem = pl.BlockSpec(memory_space=pltpu.VMEM)
    return pl.pallas_call(
        functools.partial(totals_kernel, n_inner, n_outer),
        out_shape=jax.ShapeDtypeStruct(stats.shape, F32),
        in_specs=[vmem],
        out_specs=vmem,
        scratch_shapes=[
            pltpu.VMEM((n_outer,) + stats.shape, F32),
            pltpu.VMEM((n_inner,) + stats.shape, F32),
            pltpu.VMEM(stats.shape, F32),
            pltpu.SemaphoreType.DMA((partners,)),
            pltpu.SemaphoreType.DMA((partners,)),
        ],
        compiler_params=pltpu.CompilerParams(collective_id=1, has_side_effects=True),
    )(stats)


def finish_kernel(
    node_ref, totals_ref, combined_ref, w1_ref, gamma_ref, beta_ref, w2_ref, bias_ref, out_ref
):
    rows = out_ref.shape[0]
    filled = node_ref[0]
    count = totals_ref[2:3, :]
    mean = totals_ref[0:1, :] / count
    variance = totals_ref[1:2, :] / count - mean * mean
    scale = gamma_ref[...] * lax.rsqrt(variance + EPSILON)
    first = jnp.dot(combined_ref[...], w1_ref[...], preferred_element_type=F32)
    normed = jnp.maximum(scale * (first - mean) + beta_ref[...], 0.0).astype(BF16)
    output = jnp.dot(normed, w2_ref[...], preferred_element_type=F32) + bias_ref[...]
    row_ids = lax.broadcasted_iota(jnp.int32, output.shape, 0)
    live = row_ids < filled - pl.program_id(0) * rows
    out_ref[...] = jnp.where(live, output, 0.0).astype(BF16)


def finish(node_count, totals, combined, w_first, gamma, beta, w_second, b_second):
    nodes, width = combined.shape
    hidden = w_first.shape[1]
    rows = nodes // 8
    whole = lambda s, *_: (0, 0)
    return pl.pallas_call(
        finish_kernel,
        grid_spec=pltpu.PrefetchScalarGridSpec(
            num_scalar_prefetch=1,
            grid=(nodes // rows,),
            in_specs=[
                pl.BlockSpec(totals.shape, whole),
                pl.BlockSpec((rows, width), lambda s, *_: (s, 0)),
                pl.BlockSpec(w_first.shape, whole),
                pl.BlockSpec((1, hidden), whole),
                pl.BlockSpec((1, hidden), whole),
                pl.BlockSpec(w_second.shape, whole),
                pl.BlockSpec((1, width), whole),
            ],
            out_specs=pl.BlockSpec((rows, width), lambda s, *_: (s, 0)),
        ),
        out_shape=jax.ShapeDtypeStruct((nodes, width), BF16),
        compiler_params=pltpu.CompilerParams(vmem_limit_bytes=40 << 20),
    )(
        node_count,
        totals,
        combined,
        w_first,
        gamma.reshape(1, -1),
        beta.reshape(1, -1),
        w_second,
        b_second.reshape(1, -1),
    )


def local(
    mesh_sizes,
    features,
    tiles,
    tile_src,
    tile_count,
    node_count,
    boundary,
    send_inner,
    count_inner,
    send_outer,
    count_outer,
    w_first,
    gamma,
    beta,
    w_second,
    b_second,
):
    nblocks, _, rows = tiles.shape[:3]
    blocks = features.reshape(nblocks, rows, features.shape[1])
    recv, part = exchange(
        mesh_sizes, tile_src, tile_count, node_count, boundary, send_inner, send_outer, blocks, tiles
    )
    combined, stats = remote_tiles(tile_src, tile_count, node_count, recv, tiles, part, w_first)
    totals = all_totals(mesh_sizes, stats)
    return finish(node_count, totals, combined, w_first, gamma, beta, w_second, b_second)


def solution(mesh):
    both = ("inner", "outer")
    in_specs = (
        P(both, None),
        P(both, None, None, None),
        P(both, None),
        P(both),
        P(both),
        P(both, None),
        P(both, None, None),
        P(both, None),
        P(both, None, None),
        P(both, None),
        P(),
        P(),
        P(),
        P(),
        P(),
    )
    sizes = (mesh.shape["inner"], mesh.shape["outer"])
    return jax.shard_map(
        functools.partial(local, sizes),
        mesh=mesh,
        in_specs=in_specs,
        out_specs=P(both, None),
        check_vma=False,
    )
```

```python
import functools

import jax
import jax.numpy as jnp
from jax import lax
from jax.experimental import pallas as pl
from jax.experimental.pallas import tpu as pltpu
from jax.sharding import PartitionSpec as P

EPSILON = 1e-05
MESH = pl.DeviceIdType.MESH
BF16 = jnp.bfloat16
F32 = jnp.float32
DEPTH = 4
GROUP = 8


def peers_of(n_inner, n_outer):
    i, o = lax.axis_index("inner"), lax.axis_index("outer")
    inner = [((lax.rem(i + k, n_inner), o), k) for k in range(1, n_inner)]
    outer = [((i, lax.rem(o + k, n_outer)), k) for k in range(1, n_outer)]
    return inner, outer


def enter(partners):
    barrier = pltpu.get_barrier_semaphore()
    for device, _ in partners:
        pl.semaphore_signal(barrier, inc=1, device_id=device, device_id_type=MESH)
    pl.semaphore_wait(barrier, len(partners))


def exchange_kernel(
    n_inner,
    n_outer,
    node_ref,
    src_hbm,
    count_hbm,
    border_hbm,
    send_in_hbm,
    send_out_hbm,
    feat_ref,
    tile_ref,
    recv_ref,
    part_ref,
    table,
    masks,
    packed,
    tile_buf,
    part_buf,
    src_ref,
    count_ref,
    border_ref,
    send_in_ref,
    send_out_ref,
    feat_sem,
    zero_sem,
    list_sem,
    tile_sem,
    part_sem,
    send_sem,
    recv_sem,
):
    nb, per_block, rows = tile_ref.shape[0], tile_ref.shape[1], tile_ref.shape[2]
    width = feat_ref.shape[2]
    cap = send_in_ref.shape[2]
    i, o = lax.axis_index("inner"), lax.axis_index("outer")
    inner, outer = peers_of(n_inner, n_outer)
    filled = node_ref[0]
    steps = nb // DEPTH

    lists = [
        pltpu.make_async_copy(source, target, list_sem.at[at])
        for at, (source, target) in enumerate(
            (
                (border_hbm, border_ref),
                (send_in_hbm, send_in_ref),
                (send_out_hbm, send_out_ref),
                (src_hbm, src_ref),
                (count_hbm, count_ref),
            )
        )
    ]
    for copy in lists:
        copy.start()
    feats = pltpu.make_async_copy(feat_ref, table.at[pl.ds(0, nb)], feat_sem)
    feats.start()

    def tile_copy(g, slot):
        return pltpu.make_async_copy(
            tile_ref.at[pl.ds(g * DEPTH, DEPTH)], tile_buf.at[slot], tile_sem.at[slot]
        )

    def part_copy(g, slot):
        return pltpu.make_async_copy(
            part_buf.at[slot], part_ref.at[pl.ds(g * DEPTH, DEPTH)], part_sem.at[slot]
        )

    row_ids = lax.broadcasted_iota(jnp.int32, (rows, width), 0)
    masks[0] = jnp.ones((rows, width), BF16)
    masks[1] = jnp.where(row_ids < lax.rem(filled, rows), 1.0, 0.0).astype(BF16)
    masks[2] = jnp.zeros((rows, width), BF16)
    table[nb] = jnp.zeros((rows, width), BF16)
    enter(inner + outer)
    for copy in lists:
        copy.wait()
    feats.wait()

    def live_block(block):
        above = (block * rows >= filled).astype(jnp.int32)
        partly = (block * rows + rows > filled).astype(jnp.int32)
        return table[block] * masks[above + partly]

    copies = []
    order = []
    for k in range(max(n_inner, n_outer)):
        if k < len(inner):
            order.append((inner[k], True))
        if k < len(outer):
            order.append((outer[k], False))
    for at, ((device, step), is_inner) in enumerate(order):
        for c in range(cap):
            if is_inner:
                entry = send_in_ref[0, device[0], c]
            else:
                entry = send_out_ref[0, c, device[1]]
            packed[at, c] = live_block(border_ref[0, entry])
        first_slot = i * cap if is_inner else (n_inner + o) * cap
        copy = pltpu.make_async_remote_copy(
            src_ref=packed.at[at],
            dst_ref=recv_ref.at[pl.ds(first_slot, cap)],
            send_sem=send_sem.at[at],
            recv_sem=recv_sem.at[at],
            device_id=device,
            device_id_type=MESH,
        )
        copy.start()
        copies.append(copy)

    for g in range(2):
        tile_copy(g, g).start()

    @pl.loop(0, nb // 4)
    def _(at):
        for d in range(4):
            table[at * 4 + d] = live_block(at * 4 + d)

    last = recv_ref.shape[0] - 1
    zeros = pltpu.make_async_copy(table.at[nb], recv_ref.at[last], zero_sem)
    zeros.start()

    @pl.loop(0, steps)
    def _(g):
        slot = lax.rem(g, 2)
        tile_copy(g, slot).wait()

        @pl.when(g >= 2)
        def _():
            part_copy(g - 2, slot).wait()

        for d in range(DEPTH):
            b = g * DEPTH + d
            used = count_ref[b]
            total = table[b].astype(F32)
            for pair in range(per_block // 2):
                weights, sources = [], []
                for j in (2 * pair, 2 * pair + 1):
                    s = src_ref[j, b]
                    ok = jnp.logical_and(s < nb, j < used)
                    sources.append(table[jnp.where(ok, s, nb)])
                    weights.append(tile_buf[slot, d, j])
                total += jnp.dot(
                    jnp.concatenate(weights, axis=1),
                    jnp.concatenate(sources, axis=0),
                    preferred_element_type=F32,
                )
            part_buf[slot, d] = total
        part_copy(g, slot).start()

        @pl.when(g + 2 < steps)
        def _():
            tile_copy(g + 2, slot).start()

    for g in (steps - 2, steps - 1):
        part_copy(g, g % 2).wait()
    zeros.wait()
    for copy in copies:
        copy.wait()


def exchange(mesh_sizes, tile_src, tile_count, node_count, boundary, send_inner, send_outer, blocks, tiles):
    n_inner, n_outer = mesh_sizes
    nb, per_block, rows = tiles.shape[:3]
    width = blocks.shape[2]
    cap = send_inner.shape[2]
    slots = (n_inner + n_outer) * cap + 1
    partners = n_inner + n_outer - 2
    smem = pl.BlockSpec(memory_space=pltpu.SMEM)
    hbm = pl.BlockSpec(memory_space=pltpu.HBM)
    free = pl.BlockSpec(memory_space=pl.ANY)
    return pl.pallas_call(
        functools.partial(exchange_kernel, n_inner, n_outer),
        out_shape=(
            jax.ShapeDtypeStruct((slots, rows, width), BF16),
            jax.ShapeDtypeStruct((nb, rows, width), F32),
        ),
        in_specs=[smem] + [hbm] * 7,
        out_specs=(free, free),
        scratch_shapes=[
            pltpu.VMEM((nb + 1, rows, width), BF16),
            pltpu.VMEM((3, rows, width), BF16),
            pltpu.VMEM((partners, cap, rows, width), BF16),
            pltpu.VMEM((2, DEPTH, per_block, rows, rows), BF16),
            pltpu.VMEM((2, DEPTH, rows, width), F32),
            pltpu.SMEM(tile_src.shape, jnp.int32),
            pltpu.SMEM(tile_count.shape, jnp.int32),
            pltpu.SMEM(boundary.shape, jnp.int32),
            pltpu.SMEM(send_inner.shape, jnp.int32),
            pltpu.SMEM(send_outer.shape, jnp.int32),
            pltpu.SemaphoreType.DMA,
            pltpu.SemaphoreType.DMA,
            pltpu.SemaphoreType.DMA((5,)),
            pltpu.SemaphoreType.DMA((2,)),
            pltpu.SemaphoreType.DMA((2,)),
            pltpu.SemaphoreType.DMA((partners,)),
            pltpu.SemaphoreType.DMA((partners,)),
        ],
        compiler_params=pltpu.CompilerParams(
            collective_id=0, has_side_effects=True, vmem_limit_bytes=18 << 20
        ),
    )(
        node_count,
        *(
            pltpu.with_memory_space_constraint(x, pltpu.HBM)
            for x in (tile_src, tile_count, boundary, send_inner, send_outer, blocks, tiles)
        ),
    )


def remote_kernel(
    src_ref, count_ref, node_ref, recv_ref, tile_ref, part_ref, w_ref, out_ref, stats_ref
):
    step = pl.program_id(0)
    nb_all = src_ref.shape[1]
    group, per_block, rows = tile_ref.shape[:3]
    width = part_ref.shape[2]
    zero_slot = recv_ref.shape[0] - 1
    filled = node_ref[0]

    @pl.when(step == 0)
    def _():
        stats_ref[...] = jnp.zeros_like(stats_ref)

    found = []
    for g in range(group):
        b = step * group + g
        used = count_ref[b]
        code, n = jnp.int32(0), jnp.int32(0)
        for j in range(per_block):
            hit = jnp.logical_and(src_ref[j, b] >= nb_all, j < used).astype(jnp.int32)
            code = code + hit * jnp.left_shift(jnp.int32(j), 3 * n)
            n = n + hit
        found.append((b, code, n))

    def pair_product(g, pair):
        b, code, n = found[g]
        weights, sources = [], []
        for rank in (2 * pair, 2 * pair + 1):
            j = jnp.bitwise_and(jnp.right_shift(code, 3 * rank), 7)
            slot = jnp.where(rank < n, src_ref[j, b] - nb_all, zero_slot)
            sources.append(recv_ref[slot])
            weights.append(tile_ref[g, j])
        return jnp.dot(
            jnp.concatenate(weights, axis=1),
            jnp.concatenate(sources, axis=0),
            preferred_element_type=F32,
        )

    for g in range(group):
        part_ref[g] += pair_product(g, 0)
    for g in range(group):
        for pair in range(1, per_block // 2):

            @pl.when(found[g][2] > 2 * pair)
            def _():
                part_ref[g] += pair_product(g, pair)

    combined = part_ref[...].reshape(group * rows, width).astype(BF16)
    out_ref[...] = combined
    first = jnp.dot(combined, w_ref[...], preferred_element_type=F32)
    halves = first.shape[1] // 128
    rows_left = filled - step * group * rows

    def add_sums(kept):
        for at, value in enumerate((kept, kept * kept)):
            line = jnp.sum(value, axis=0, keepdims=True)
            for h in range(halves):
                spot = at * halves + h
                stats_ref[spot : spot + 1, :] += line[:, h * 128 : (h + 1) * 128]

    @pl.when(rows_left >= group * rows)
    def _():
        add_sums(first)

    @pl.when(jnp.logical_and(rows_left > 0, rows_left < group * rows))
    def _():
        row_ids = lax.broadcasted_iota(jnp.int32, first.shape, 0)
        add_sums(jnp.where(row_ids < rows_left, first, 0.0))

    @pl.when(step == 0)
    def _():
        spot = 2 * halves
        stats_ref[spot : spot + 1, :] = jnp.full((1, 128), filled.astype(F32))


def remote_tiles(tile_src, tile_count, node_count, recv, tiles, part, w_first):
    nb, per_block, rows = tiles.shape[:3]
    width = part.shape[2]
    lines = -(-(2 * (w_first.shape[1] // 128) + 1) // 8) * 8
    return pl.pallas_call(
        remote_kernel,
        grid_spec=pltpu.PrefetchScalarGridSpec(
            num_scalar_prefetch=3,
            grid=(nb // GROUP,),
            in_specs=[
                pl.BlockSpec(recv.shape, lambda s, *_: (0, 0, 0)),
                pl.BlockSpec((GROUP, per_block, rows, rows), lambda s, *_: (s, 0, 0, 0)),
                pl.BlockSpec((GROUP, rows, width), lambda s, *_: (s, 0, 0)),
                pl.BlockSpec(w_first.shape, lambda s, *_: (0, 0)),
            ],
            out_specs=[
                pl.BlockSpec((GROUP * rows, width), lambda s, *_: (s, 0)),
                pl.BlockSpec((lines, 128), lambda s, *_: (0, 0)),
            ],
        ),
        out_shape=(
            jax.ShapeDtypeStruct((nb * rows, width), BF16),
            jax.ShapeDtypeStruct((lines, 128), F32),
        ),
        compiler_params=pltpu.CompilerParams(vmem_limit_bytes=20 << 20),
    )(tile_src, tile_count, node_count, recv, tiles, part, w_first)


def totals_kernel(n_inner, n_outer, stats_ref, out_ref, first_buf, second_buf, mid, send_sem, recv_sem):
    i, o = lax.axis_index("inner"), lax.axis_index("outer")
    inner, outer = peers_of(n_inner, n_outer)
    enter(inner + outer)

    def round_of(partners, source, buf, me, base):
        copies = []
        for at, (device, _) in enumerate(partners):
            copy = pltpu.make_async_remote_copy(
                src_ref=source,
                dst_ref=buf.at[me],
                send_sem=send_sem.at[base + at],
                recv_sem=recv_sem.at[base + at],
                device_id=device,
                device_id_type=MESH,
            )
            copy.start()
            copies.append(copy)
        buf[me] = source[...]
        for copy in copies:
            copy.wait()
        return jnp.sum(buf[...], axis=0)

    mid[...] = round_of(outer, stats_ref, first_buf, o, 0)
    out_ref[...] = round_of(inner, mid, second_buf, i, len(outer))


def all_totals(mesh_sizes, stats):
    n_inner, n_outer = mesh_sizes
    partners = n_inner + n_outer - 2
    vmem = pl.BlockSpec(memory_space=pltpu.VMEM)
    return pl.pallas_call(
        functools.partial(totals_kernel, n_inner, n_outer),
        out_shape=jax.ShapeDtypeStruct(stats.shape, F32),
        in_specs=[vmem],
        out_specs=vmem,
        scratch_shapes=[
            pltpu.VMEM((n_outer,) + stats.shape, F32),
            pltpu.VMEM((n_inner,) + stats.shape, F32),
            pltpu.VMEM(stats.shape, F32),
            pltpu.SemaphoreType.DMA((partners,)),
            pltpu.SemaphoreType.DMA((partners,)),
        ],
        compiler_params=pltpu.CompilerParams(collective_id=1, has_side_effects=True, vmem_limit_bytes=2 << 20),
    )(stats)


def finish_kernel(
    node_ref, totals_ref, combined_ref, w1_ref, gamma_ref, beta_ref, w2_ref, bias_ref, out_ref
):
    rows = out_ref.shape[0]
    filled = node_ref[0]
    halves = gamma_ref.shape[1] // 128

    def line(first_row):
        parts = [totals_ref[first_row + h : first_row + h + 1, :] for h in range(halves)]
        return jnp.concatenate(parts, axis=1)

    count = totals_ref[2 * halves : 2 * halves + 1, 0:1]
    mean = line(0) / count
    variance = line(halves) / count - mean * mean
    scale = gamma_ref[...] * lax.rsqrt(variance + EPSILON)
    rows_left = filled - pl.program_id(0) * rows

    def result():
        first = jnp.dot(combined_ref[...], w1_ref[...], preferred_element_type=F32)
        normed = jnp.maximum(scale * (first - mean) + beta_ref[...], 0.0).astype(BF16)
        return jnp.dot(normed, w2_ref[...], preferred_element_type=F32) + bias_ref[...]

    @pl.when(rows_left >= rows)
    def _():
        out_ref[...] = result().astype(BF16)

    @pl.when(rows_left < rows)
    def _():
        output = result()
        row_ids = lax.broadcasted_iota(jnp.int32, output.shape, 0)
        out_ref[...] = jnp.where(row_ids < rows_left, output, 0.0).astype(BF16)


def finish(node_count, totals, combined, w_first, gamma, beta, w_second, b_second):
    nodes, width = combined.shape
    hidden = w_first.shape[1]
    rows = nodes // 8
    whole = lambda s, *_: (0, 0)
    return pl.pallas_call(
        finish_kernel,
        grid_spec=pltpu.PrefetchScalarGridSpec(
            num_scalar_prefetch=1,
            grid=(nodes // rows,),
            in_specs=[
                pl.BlockSpec(totals.shape, whole),
                pl.BlockSpec((rows, width), lambda s, *_: (s, 0)),
                pl.BlockSpec(w_first.shape, whole),
                pl.BlockSpec((1, hidden), whole),
                pl.BlockSpec((1, hidden), whole),
                pl.BlockSpec(w_second.shape, whole),
                pl.BlockSpec((1, width), whole),
            ],
            out_specs=pl.BlockSpec((rows, width), lambda s, *_: (s, 0)),
        ),
        out_shape=jax.ShapeDtypeStruct((nodes, width), BF16),
        compiler_params=pltpu.CompilerParams(vmem_limit_bytes=20 << 20),
    )(
        node_count,
        totals,
        combined,
        w_first,
        gamma.reshape(1, -1),
        beta.reshape(1, -1),
        w_second,
        b_second.reshape(1, -1),
    )


def local(
    mesh_sizes,
    features,
    tiles,
    tile_src,
    tile_count,
    node_count,
    boundary,
    send_inner,
    count_inner,
    send_outer,
    count_outer,
    w_first,
    gamma,
    beta,
    w_second,
    b_second,
):
    nblocks, _, rows = tiles.shape[:3]
    blocks = features.reshape(nblocks, rows, features.shape[1])
    tile_src = tile_src.T
    send_outer = send_outer.transpose(0, 2, 1)
    tiles = pltpu.with_memory_space_constraint(tiles, pltpu.HBM)
    recv, part = exchange(
        mesh_sizes, tile_src, tile_count, node_count, boundary, send_inner, send_outer, blocks, tiles
    )
    combined, stats = remote_tiles(tile_src, tile_count, node_count, recv, tiles, part, w_first)
    totals = all_totals(mesh_sizes, stats)
    return finish(node_count, totals, combined, w_first, gamma, beta, w_second, b_second)


def solution(mesh):
    both = ("inner", "outer")
    in_specs = (
        P(both, None),
        P(both, None, None, None),
        P(both, None),
        P(both),
        P(both),
        P(both, None),
        P(both, None, None),
        P(both, None),
        P(both, None, None),
        P(both, None),
        P(),
        P(),
        P(),
        P(),
        P(),
    )
    sizes = (mesh.shape["inner"], mesh.shape["outer"])
    return jax.shard_map(
        functools.partial(local, sizes),
        mesh=mesh,
        in_specs=in_specs,
        out_specs=P(both, None),
        check_vma=False,
    )
```

```python
import functools

import jax
import jax.numpy as jnp
from jax import lax
from jax.experimental import pallas as pl
from jax.experimental.pallas import tpu as pltpu
from jax.sharding import PartitionSpec as P

EPSILON = 1e-05
MESH = pl.DeviceIdType.MESH
BF16 = jnp.bfloat16
F32 = jnp.float32
DEPTH = 4
BATCH = 4
REMOTE_LIMIT = 32
FINISH_LIMIT = 16
GROUP = 8


def peers_of(n_inner, n_outer):
    i, o = lax.axis_index("inner"), lax.axis_index("outer")
    inner = [((lax.rem(i + k, n_inner), o), k) for k in range(1, n_inner)]
    outer = [((i, lax.rem(o + k, n_outer)), k) for k in range(1, n_outer)]
    return inner, outer


def enter(partners):
    barrier = pltpu.get_barrier_semaphore()
    for device, _ in partners:
        pl.semaphore_signal(barrier, inc=1, device_id=device, device_id_type=MESH)
    pl.semaphore_wait(barrier, len(partners))


def exchange_kernel(
    n_inner,
    n_outer,
    node_ref,
    src_hbm,
    count_hbm,
    border_hbm,
    send_in_hbm,
    send_out_hbm,
    feat_ref,
    tile_ref,
    recv_ref,
    part_ref,
    table,
    masks,
    packed,
    tile_buf,
    part_buf,
    src_ref,
    count_ref,
    border_ref,
    send_in_ref,
    send_out_ref,
    feat_sem,
    zero_sem,
    list_sem,
    tile_sem,
    part_sem,
    send_sem,
    recv_sem,
):
    nb, per_block, rows = tile_ref.shape[0], tile_ref.shape[1], tile_ref.shape[2]
    width = feat_ref.shape[2]
    cap = send_in_ref.shape[2]
    i, o = lax.axis_index("inner"), lax.axis_index("outer")
    inner, outer = peers_of(n_inner, n_outer)
    filled = node_ref[0]
    steps = nb // DEPTH

    lists = [
        pltpu.make_async_copy(source, target, list_sem.at[at])
        for at, (source, target) in enumerate(
            (
                (border_hbm, border_ref),
                (send_in_hbm, send_in_ref),
                (send_out_hbm, send_out_ref),
                (src_hbm, src_ref),
                (count_hbm, count_ref),
            )
        )
    ]
    for copy in lists:
        copy.start()
    feats = pltpu.make_async_copy(feat_ref, table.at[pl.ds(0, nb)], feat_sem)
    feats.start()

    def tile_copy(g, slot):
        return pltpu.make_async_copy(
            tile_ref.at[pl.ds(g * DEPTH, DEPTH)], tile_buf.at[slot], tile_sem.at[slot]
        )

    def part_copy(g, slot):
        return pltpu.make_async_copy(
            part_buf.at[slot], part_ref.at[pl.ds(g * DEPTH, DEPTH)], part_sem.at[slot]
        )

    row_ids = lax.broadcasted_iota(jnp.int32, (rows, width), 0)
    masks[0] = jnp.ones((rows, width), BF16)
    masks[1] = jnp.where(row_ids < lax.rem(filled, rows), 1.0, 0.0).astype(BF16)
    masks[2] = jnp.zeros((rows, width), BF16)
    table[nb] = jnp.zeros((rows, width), BF16)
    enter(inner + outer)
    for copy in lists:
        copy.wait()
    feats.wait()

    def live_block(block):
        above = (block * rows >= filled).astype(jnp.int32)
        partly = (block * rows + rows > filled).astype(jnp.int32)
        return table[block] * masks[above + partly]

    copies = []
    order = []
    for k in range(max(n_inner, n_outer)):
        if k < len(inner):
            order.append((inner[k], True))
        if k < len(outer):
            order.append((outer[k], False))
    for at, ((device, step), is_inner) in enumerate(order):
        for c in range(cap):
            if is_inner:
                entry = send_in_ref[0, device[0], c]
            else:
                entry = send_out_ref[0, c, device[1]]
            packed[at, c] = live_block(border_ref[0, entry])
        first_slot = i * cap if is_inner else (n_inner + o) * cap
        copy = pltpu.make_async_remote_copy(
            src_ref=packed.at[at],
            dst_ref=recv_ref.at[pl.ds(first_slot, cap)],
            send_sem=send_sem.at[at],
            recv_sem=recv_sem.at[at],
            device_id=device,
            device_id_type=MESH,
        )
        copy.start()
        copies.append(copy)

    for g in range(2):
        tile_copy(g, g).start()

    @pl.loop(0, nb // 4)
    def _(at):
        for d in range(4):
            table[at * 4 + d] = live_block(at * 4 + d)

    last = recv_ref.shape[0] - 1
    zeros = pltpu.make_async_copy(table.at[nb], recv_ref.at[last], zero_sem)
    zeros.start()

    @pl.loop(0, steps)
    def _(g):
        slot = lax.rem(g, 2)
        tile_copy(g, slot).wait()

        @pl.when(g >= 2)
        def _():
            part_copy(g - 2, slot).wait()

        for d in range(DEPTH):
            b = g * DEPTH + d
            used = count_ref[b]
            total = table[b].astype(F32)
            for pair in range(per_block // 2):
                weights, sources = [], []
                for j in (2 * pair, 2 * pair + 1):
                    s = src_ref[j, b]
                    ok = jnp.logical_and(s < nb, j < used)
                    sources.append(table[jnp.where(ok, s, nb)])
                    weights.append(tile_buf[slot, d, j])
                total += jnp.dot(
                    jnp.concatenate(weights, axis=1),
                    jnp.concatenate(sources, axis=0),
                    preferred_element_type=F32,
                )
            part_buf[slot, d] = total
        part_copy(g, slot).start()

        @pl.when(g + 2 < steps)
        def _():
            tile_copy(g + 2, slot).start()

    for g in (steps - 2, steps - 1):
        part_copy(g, g % 2).wait()
    zeros.wait()
    for copy in copies:
        copy.wait()


def exchange(mesh_sizes, tile_src, tile_count, node_count, boundary, send_inner, send_outer, blocks, tiles):
    n_inner, n_outer = mesh_sizes
    nb, per_block, rows = tiles.shape[:3]
    width = blocks.shape[2]
    cap = send_inner.shape[2]
    slots = (n_inner + n_outer) * cap + 1
    partners = n_inner + n_outer - 2
    smem = pl.BlockSpec(memory_space=pltpu.SMEM)
    hbm = pl.BlockSpec(memory_space=pltpu.HBM)
    free = pl.BlockSpec(memory_space=pl.ANY)
    return pl.pallas_call(
        functools.partial(exchange_kernel, n_inner, n_outer),
        out_shape=(
            jax.ShapeDtypeStruct((slots, rows, width), BF16),
            jax.ShapeDtypeStruct((nb, rows, width), F32),
        ),
        in_specs=[smem] + [hbm] * 7,
        out_specs=(free, free),
        scratch_shapes=[
            pltpu.VMEM((nb + 1, rows, width), BF16),
            pltpu.VMEM((3, rows, width), BF16),
            pltpu.VMEM((partners, cap, rows, width), BF16),
            pltpu.VMEM((2, DEPTH, per_block, rows, rows), BF16),
            pltpu.VMEM((2, DEPTH, rows, width), F32),
            pltpu.SMEM(tile_src.shape, jnp.int32),
            pltpu.SMEM(tile_count.shape, jnp.int32),
            pltpu.SMEM(boundary.shape, jnp.int32),
            pltpu.SMEM(send_inner.shape, jnp.int32),
            pltpu.SMEM(send_outer.shape, jnp.int32),
            pltpu.SemaphoreType.DMA,
            pltpu.SemaphoreType.DMA,
            pltpu.SemaphoreType.DMA((5,)),
            pltpu.SemaphoreType.DMA((2,)),
            pltpu.SemaphoreType.DMA((2,)),
            pltpu.SemaphoreType.DMA((partners,)),
            pltpu.SemaphoreType.DMA((partners,)),
        ],
        compiler_params=pltpu.CompilerParams(
            collective_id=0, has_side_effects=True, vmem_limit_bytes=18 << 20
        ),
    )(
        node_count,
        *(
            pltpu.with_memory_space_constraint(x, pltpu.HBM)
            for x in (tile_src, tile_count, boundary, send_inner, send_outer, blocks, tiles)
        ),
    )


def remote_kernel(
    src_ref,
    count_ref,
    node_ref,
    recv_ref,
    tile_hbm,
    part_ref,
    w_ref,
    out_ref,
    stats_ref,
    tile_ref,
    total_ref,
    code_ref,
    found_ref,
    extra_ref,
    tile_sem,
):
    nb, per_block, rows = tile_ref.shape[:3]
    width = part_ref.shape[2]
    zero_slot = recv_ref.shape[0] - 1
    filled = node_ref[0]
    steps = nb // GROUP

    def tile_copy(step):
        some = pl.ds(step * GROUP, GROUP)
        return pltpu.make_async_copy(tile_hbm.at[some], tile_ref.at[some], tile_sem.at[step])

    for step in range(steps):
        tile_copy(step).start()

    def pair_product(b, code, n, pair):
        weights, sources = [], []
        for at in range(2):
            rank = 2 * pair + at
            j = jnp.bitwise_and(jnp.right_shift(code, 3 * rank), 7)
            slot = jnp.where(rank < n, src_ref[j, b] - nb, zero_slot)
            sources.append(recv_ref[slot])
            weights.append(tile_ref[b, j])
        return jnp.dot(
            jnp.concatenate(weights, axis=1),
            jnp.concatenate(sources, axis=0),
            preferred_element_type=F32,
        )

    def first_pairs(step, extra):
        tile_copy(step).wait()
        for g in range(GROUP):
            b = step * GROUP + g
            used = count_ref[b]
            code, n = jnp.int32(0), jnp.int32(0)
            for j in range(per_block):
                hit = jnp.logical_and(src_ref[j, b] >= nb, j < used).astype(jnp.int32)
                code = code + hit * jnp.left_shift(jnp.int32(j), 3 * n)
                n = n + hit
            code_ref[b] = code
            found_ref[b] = n
            for pair in range(1, per_block // 2):
                extra_ref[extra] = b * 8 + pair
                extra = extra + (n > 2 * pair).astype(jnp.int32)
            total_ref[b] = part_ref[b] + pair_product(b, code, n, 0)
        return extra

    extra = lax.fori_loop(0, steps, first_pairs, jnp.int32(0))
    for at in range(BATCH):
        extra_ref[extra + at] = per_block // 2

    @pl.loop(0, (extra + BATCH - 1) // BATCH)
    def _(turn):
        products = []
        for at in range(BATCH):
            item = extra_ref[turn * BATCH + at]
            b = item // 8
            products.append((b, pair_product(b, code_ref[b], found_ref[b], lax.rem(item, 8))))
        for b, product in products:
            total_ref[b] += product

    halves = w_ref.shape[1] // 128
    stats_ref[...] = jnp.zeros_like(stats_ref)
    stats_ref[2 * halves : 2 * halves + 1, :] = jnp.full((1, 128), filled.astype(F32))

    @pl.loop(0, steps)
    def _(step):
        blocks = pl.ds(step * GROUP, GROUP)
        combined = total_ref[blocks].reshape(GROUP * rows, width).astype(BF16)
        out_ref[pl.ds(step * (GROUP * rows), GROUP * rows)] = combined
        first = jnp.dot(combined, w_ref[...], preferred_element_type=F32)
        rows_left = filled - step * (GROUP * rows)

        def add_sums(kept):
            for at, value in enumerate((kept, kept * kept)):
                line = jnp.sum(value, axis=0, keepdims=True)
                for h in range(halves):
                    spot = at * halves + h
                    stats_ref[spot : spot + 1, :] += line[:, h * 128 : (h + 1) * 128]

        @pl.when(rows_left >= GROUP * rows)
        def _():
            add_sums(first)

        @pl.when(jnp.logical_and(rows_left > 0, rows_left < GROUP * rows))
        def _():
            row_ids = lax.broadcasted_iota(jnp.int32, first.shape, 0)
            add_sums(jnp.where(row_ids < rows_left, first, 0.0))


def remote_tiles(tile_src, tile_count, node_count, recv, tiles, part, w_first):
    nb, per_block, rows = tiles.shape[:3]
    width = part.shape[2]
    lines = -(-(2 * (w_first.shape[1] // 128) + 1) // 8) * 8
    smem = pl.BlockSpec(memory_space=pltpu.SMEM)
    vmem = pl.BlockSpec(memory_space=pltpu.VMEM)
    hbm = pl.BlockSpec(memory_space=pltpu.HBM)
    return pl.pallas_call(
        remote_kernel,
        in_specs=[smem, smem, smem, vmem, hbm, vmem, vmem],
        out_specs=(vmem, vmem),
        out_shape=(
            jax.ShapeDtypeStruct((nb * rows, width), BF16),
            jax.ShapeDtypeStruct((lines, 128), F32),
        ),
        scratch_shapes=[
            pltpu.VMEM(tiles.shape, BF16),
            pltpu.VMEM((nb, rows, width), F32),
            pltpu.SMEM((nb,), jnp.int32),
            pltpu.SMEM((nb,), jnp.int32),
            pltpu.SMEM((nb * per_block // 2 + BATCH,), jnp.int32),
            pltpu.SemaphoreType.DMA((nb // GROUP,)),
        ],
        compiler_params=pltpu.CompilerParams(vmem_limit_bytes=REMOTE_LIMIT << 20),
    )(
        tile_src,
        tile_count,
        node_count,
        recv,
        pltpu.with_memory_space_constraint(tiles, pltpu.HBM),
        part,
        w_first,
    )


def totals_kernel(n_inner, n_outer, stats_ref, out_ref, first_buf, second_buf, mid, send_sem, recv_sem):
    i, o = lax.axis_index("inner"), lax.axis_index("outer")
    inner, outer = peers_of(n_inner, n_outer)
    enter(inner + outer)

    def round_of(partners, source, buf, me, base):
        copies = []
        for at, (device, _) in enumerate(partners):
            copy = pltpu.make_async_remote_copy(
                src_ref=source,
                dst_ref=buf.at[me],
                send_sem=send_sem.at[base + at],
                recv_sem=recv_sem.at[base + at],
                device_id=device,
                device_id_type=MESH,
            )
            copy.start()
            copies.append(copy)
        buf[me] = source[...]
        for copy in copies:
            copy.wait()
        return jnp.sum(buf[...], axis=0)

    mid[...] = round_of(outer, stats_ref, first_buf, o, 0)
    out_ref[...] = round_of(inner, mid, second_buf, i, len(outer))


def all_totals(mesh_sizes, stats):
    n_inner, n_outer = mesh_sizes
    partners = n_inner + n_outer - 2
    vmem = pl.BlockSpec(memory_space=pltpu.VMEM)
    return pl.pallas_call(
        functools.partial(totals_kernel, n_inner, n_outer),
        out_shape=jax.ShapeDtypeStruct(stats.shape, F32),
        in_specs=[vmem],
        out_specs=vmem,
        scratch_shapes=[
            pltpu.VMEM((n_outer,) + stats.shape, F32),
            pltpu.VMEM((n_inner,) + stats.shape, F32),
            pltpu.VMEM(stats.shape, F32),
            pltpu.SemaphoreType.DMA((partners,)),
            pltpu.SemaphoreType.DMA((partners,)),
        ],
        compiler_params=pltpu.CompilerParams(collective_id=1, has_side_effects=True, vmem_limit_bytes=2 << 20),
    )(stats)


def finish_kernel(
    node_ref,
    totals_ref,
    combined_ref,
    w1_ref,
    gamma_ref,
    beta_ref,
    w2_ref,
    bias_ref,
    out_hbm,
    stage,
    out_sem,
):
    rows = stage.shape[1]
    steps = out_hbm.shape[0] // rows
    filled = node_ref[0]
    halves = gamma_ref.shape[1] // 128

    def line(first_row):
        parts = [totals_ref[first_row + h : first_row + h + 1, :] for h in range(halves)]
        return jnp.concatenate(parts, axis=1)

    count = totals_ref[2 * halves : 2 * halves + 1, 0:1]
    mean = line(0) / count
    variance = line(halves) / count - mean * mean
    scale = gamma_ref[...] * lax.rsqrt(variance + EPSILON)

    def out_copy(step, slot):
        return pltpu.make_async_copy(
            stage.at[slot], out_hbm.at[pl.ds(step * rows, rows)], out_sem.at[slot]
        )

    @pl.loop(0, steps)
    def _(step):
        slot = lax.rem(step, 2)
        rows_left = filled - step * rows

        @pl.when(step >= 2)
        def _():
            out_copy(step - 2, slot).wait()

        def result():
            combined = combined_ref[pl.ds(step * rows, rows)]
            first = jnp.dot(combined, w1_ref[...], preferred_element_type=F32)
            normed = jnp.maximum(scale * (first - mean) + beta_ref[...], 0.0).astype(BF16)
            return jnp.dot(normed, w2_ref[...], preferred_element_type=F32) + bias_ref[...]

        @pl.when(rows_left >= rows)
        def _():
            stage[slot] = result().astype(BF16)

        @pl.when(jnp.logical_and(rows_left > 0, rows_left < rows))
        def _():
            output = result()
            row_ids = lax.broadcasted_iota(jnp.int32, output.shape, 0)
            stage[slot] = jnp.where(row_ids < rows_left, output, 0.0).astype(BF16)

        @pl.when(rows_left <= 0)
        def _():
            stage[slot] = jnp.zeros(stage.shape[1:], BF16)

        out_copy(step, slot).start()

    for step in (steps - 2, steps - 1):
        out_copy(step, step % 2).wait()


def finish(node_count, totals, combined, w_first, gamma, beta, w_second, b_second):
    nodes, width = combined.shape
    rows = nodes // 8
    smem = pl.BlockSpec(memory_space=pltpu.SMEM)
    vmem = pl.BlockSpec(memory_space=pltpu.VMEM)
    return pl.pallas_call(
        finish_kernel,
        in_specs=[smem] + [vmem] * 7,
        out_specs=pl.BlockSpec(memory_space=pltpu.HBM),
        out_shape=jax.ShapeDtypeStruct((nodes, width), BF16),
        scratch_shapes=[pltpu.VMEM((2, rows, width), BF16), pltpu.SemaphoreType.DMA((2,))],
        compiler_params=pltpu.CompilerParams(vmem_limit_bytes=FINISH_LIMIT << 20),
    )(
        node_count,
        totals,
        combined,
        w_first,
        gamma.reshape(1, -1),
        beta.reshape(1, -1),
        w_second,
        b_second.reshape(1, -1),
    )


def local(
    mesh_sizes,
    features,
    tiles,
    tile_src,
    tile_count,
    node_count,
    boundary,
    send_inner,
    count_inner,
    send_outer,
    count_outer,
    w_first,
    gamma,
    beta,
    w_second,
    b_second,
):
    nblocks, _, rows = tiles.shape[:3]
    blocks = features.reshape(nblocks, rows, features.shape[1])
    tile_src = tile_src.T
    send_outer = send_outer.transpose(0, 2, 1)
    recv, part = exchange(
        mesh_sizes, tile_src, tile_count, node_count, boundary, send_inner, send_outer, blocks, tiles
    )
    combined, stats = remote_tiles(tile_src, tile_count, node_count, recv, tiles, part, w_first)
    totals = all_totals(mesh_sizes, stats)
    return finish(node_count, totals, combined, w_first, gamma, beta, w_second, b_second)


def solution(mesh):
    both = ("inner", "outer")
    in_specs = (
        P(both, None),
        P(both, None, None, None),
        P(both, None),
        P(both),
        P(both),
        P(both, None),
        P(both, None, None),
        P(both, None),
        P(both, None, None),
        P(both, None),
        P(),
        P(),
        P(),
        P(),
        P(),
    )
    sizes = (mesh.shape["inner"], mesh.shape["outer"])
    return jax.shard_map(
        functools.partial(local, sizes),
        mesh=mesh,
        in_specs=in_specs,
        out_specs=P(both, None),
        check_vma=False,
    )
```

```python
import functools

import jax
import jax.numpy as jnp
from jax import lax
from jax.experimental import pallas as pl
from jax.experimental.pallas import tpu as pltpu
from jax.sharding import PartitionSpec as P

EPSILON = 1e-05
MESH = pl.DeviceIdType.MESH
BF16 = jnp.bfloat16
F32 = jnp.float32
DEPTH = 4
BATCH = 4
REMOTE_LIMIT = 14
FINISH_LIMIT = 16
GROUP = 8


def peers_of(n_inner, n_outer):
    i, o = lax.axis_index("inner"), lax.axis_index("outer")
    inner = [((lax.rem(i + k, n_inner), o), k) for k in range(1, n_inner)]
    outer = [((i, lax.rem(o + k, n_outer)), k) for k in range(1, n_outer)]
    return inner, outer


def greet(partners):
    for device, _ in partners:
        pl.semaphore_signal(
            pltpu.get_barrier_semaphore(), inc=1, device_id=device, device_id_type=MESH
        )


def enter(partners):
    pl.semaphore_wait(pltpu.get_barrier_semaphore(), len(partners))


def exchange_kernel(
    n_inner,
    n_outer,
    node_ref,
    src_hbm,
    count_hbm,
    border_hbm,
    send_in_hbm,
    send_out_hbm,
    feat_ref,
    tile_ref,
    recv_ref,
    part_ref,
    table,
    masks,
    packed,
    tile_buf,
    part_buf,
    src_ref,
    count_ref,
    border_ref,
    send_in_ref,
    send_out_ref,
    feat_sem,
    zero_sem,
    list_sem,
    tile_sem,
    part_sem,
    send_sem,
    recv_sem,
):
    nb, per_block, rows = tile_ref.shape[0], tile_ref.shape[1], tile_ref.shape[2]
    width = feat_ref.shape[2]
    cap = send_in_ref.shape[2]
    i, o = lax.axis_index("inner"), lax.axis_index("outer")
    inner, outer = peers_of(n_inner, n_outer)
    filled = node_ref[0]
    steps = nb // DEPTH

    lists = [
        pltpu.make_async_copy(source, target, list_sem.at[at])
        for at, (source, target) in enumerate(
            (
                (border_hbm, border_ref),
                (send_in_hbm, send_in_ref),
                (send_out_hbm, send_out_ref),
                (src_hbm, src_ref),
                (count_hbm, count_ref),
            )
        )
    ]
    feats = pltpu.make_async_copy(feat_ref, table.at[pl.ds(0, nb)], feat_sem)
    feats.start()
    for copy in lists:
        copy.start()
    greet(inner + outer)

    def tile_copy(g, slot):
        return pltpu.make_async_copy(
            tile_ref.at[pl.ds(g * DEPTH, DEPTH)], tile_buf.at[slot], tile_sem.at[slot]
        )

    def part_copy(g, slot):
        return pltpu.make_async_copy(
            part_buf.at[slot], part_ref.at[pl.ds(g * DEPTH, DEPTH)], part_sem.at[slot]
        )

    row_ids = lax.broadcasted_iota(jnp.int32, (rows, width), 0)
    masks[0] = jnp.ones((rows, width), BF16)
    masks[1] = jnp.where(row_ids < lax.rem(filled, rows), 1.0, 0.0).astype(BF16)
    masks[2] = jnp.zeros((rows, width), BF16)
    table[nb] = jnp.zeros((rows, width), BF16)
    enter(inner + outer)
    for copy in lists:
        copy.wait()
    feats.wait()

    def live_block(block):
        above = (block * rows >= filled).astype(jnp.int32)
        partly = (block * rows + rows > filled).astype(jnp.int32)
        return table[block] * masks[above + partly]

    copies = []
    order = []
    for k in range(max(n_inner, n_outer)):
        if k < len(inner):
            order.append((inner[k], True))
        if k < len(outer):
            order.append((outer[k], False))
    for at, ((device, step), is_inner) in enumerate(order):
        for c in range(cap):
            if is_inner:
                entry = send_in_ref[0, device[0], c]
            else:
                entry = send_out_ref[0, c, device[1]]
            packed[at, c] = live_block(border_ref[0, entry])
        first_slot = i * cap if is_inner else (n_inner + o) * cap
        copy = pltpu.make_async_remote_copy(
            src_ref=packed.at[at],
            dst_ref=recv_ref.at[pl.ds(first_slot, cap)],
            send_sem=send_sem.at[at],
            recv_sem=recv_sem.at[at],
            device_id=device,
            device_id_type=MESH,
        )
        copy.start()
        copies.append(copy)

    for g in range(2):
        tile_copy(g, g).start()

    @pl.loop(0, nb // 4)
    def _(at):
        for d in range(4):
            table[at * 4 + d] = live_block(at * 4 + d)

    last = recv_ref.shape[0] - 1
    zeros = pltpu.make_async_copy(table.at[nb], recv_ref.at[last], zero_sem)
    zeros.start()

    @pl.loop(0, steps)
    def _(g):
        slot = lax.rem(g, 2)
        tile_copy(g, slot).wait()

        @pl.when(g >= 2)
        def _():
            part_copy(g - 2, slot).wait()

        for d in range(DEPTH):
            b = g * DEPTH + d
            used = count_ref[b]
            total = table[b].astype(F32)
            for pair in range(per_block // 2):
                weights, sources = [], []
                for j in (2 * pair, 2 * pair + 1):
                    s = src_ref[j, b]
                    ok = jnp.logical_and(s < nb, j < used)
                    sources.append(table[jnp.where(ok, s, nb)])
                    weights.append(tile_buf[slot, d, j])
                total += jnp.dot(
                    jnp.concatenate(weights, axis=1),
                    jnp.concatenate(sources, axis=0),
                    preferred_element_type=F32,
                )
            part_buf[slot, d] = total
        part_copy(g, slot).start()

        @pl.when(g + 2 < steps)
        def _():
            tile_copy(g + 2, slot).start()

    for g in (steps - 2, steps - 1):
        part_copy(g, g % 2).wait()
    zeros.wait()
    for copy in copies:
        copy.wait()


def exchange(mesh_sizes, tile_src, tile_count, node_count, boundary, send_inner, send_outer, blocks, tiles):
    n_inner, n_outer = mesh_sizes
    nb, per_block, rows = tiles.shape[:3]
    width = blocks.shape[2]
    cap = send_inner.shape[2]
    slots = (n_inner + n_outer) * cap + 1
    partners = n_inner + n_outer - 2
    smem = pl.BlockSpec(memory_space=pltpu.SMEM)
    hbm = pl.BlockSpec(memory_space=pltpu.HBM)
    free = pl.BlockSpec(memory_space=pl.ANY)
    return pl.pallas_call(
        functools.partial(exchange_kernel, n_inner, n_outer),
        out_shape=(
            jax.ShapeDtypeStruct((slots, rows, width), BF16),
            jax.ShapeDtypeStruct((nb, rows, width), F32),
        ),
        in_specs=[smem] + [hbm] * 7,
        out_specs=(free, free),
        scratch_shapes=[
            pltpu.VMEM((nb + 1, rows, width), BF16),
            pltpu.VMEM((3, rows, width), BF16),
            pltpu.VMEM((partners, cap, rows, width), BF16),
            pltpu.VMEM((2, DEPTH, per_block, rows, rows), BF16),
            pltpu.VMEM((2, DEPTH, rows, width), F32),
            pltpu.SMEM(tile_src.shape, jnp.int32),
            pltpu.SMEM(tile_count.shape, jnp.int32),
            pltpu.SMEM(boundary.shape, jnp.int32),
            pltpu.SMEM(send_inner.shape, jnp.int32),
            pltpu.SMEM(send_outer.shape, jnp.int32),
            pltpu.SemaphoreType.DMA,
            pltpu.SemaphoreType.DMA,
            pltpu.SemaphoreType.DMA((5,)),
            pltpu.SemaphoreType.DMA((2,)),
            pltpu.SemaphoreType.DMA((2,)),
            pltpu.SemaphoreType.DMA((partners,)),
            pltpu.SemaphoreType.DMA((partners,)),
        ],
        compiler_params=pltpu.CompilerParams(
            collective_id=0, has_side_effects=True, vmem_limit_bytes=18 << 20
        ),
    )(
        node_count,
        *(
            pltpu.with_memory_space_constraint(x, pltpu.HBM)
            for x in (tile_src, tile_count, boundary, send_inner, send_outer, blocks, tiles)
        ),
    )


def remote_kernel(
    src_ref,
    count_ref,
    node_ref,
    recv_ref,
    tile_ref,
    part_ref,
    w_ref,
    out_ref,
    stats_ref,
    total_ref,
    code_ref,
    found_ref,
    extra_ref,
):
    nb, per_block, rows = tile_ref.shape[:3]
    width = part_ref.shape[2]
    zero_slot = recv_ref.shape[0] - 1
    filled = node_ref[0]
    steps = nb // GROUP

    def pair_product(b, code, n, pair):
        weights, sources = [], []
        for at in range(2):
            rank = 2 * pair + at
            j = jnp.bitwise_and(jnp.right_shift(code, 3 * rank), 7)
            slot = jnp.where(rank < n, src_ref[j, b] - nb, zero_slot)
            sources.append(recv_ref[slot])
            weights.append(tile_ref[b, j])
        return jnp.dot(
            jnp.concatenate(weights, axis=1),
            jnp.concatenate(sources, axis=0),
            preferred_element_type=F32,
        )

    def first_pairs(step, extra):
        for g in range(GROUP):
            b = step * GROUP + g
            used = count_ref[b]
            code, n = jnp.int32(0), jnp.int32(0)
            for j in range(per_block):
                hit = jnp.logical_and(src_ref[j, b] >= nb, j < used).astype(jnp.int32)
                code = code + hit * jnp.left_shift(jnp.int32(j), 3 * n)
                n = n + hit
            code_ref[b] = code
            found_ref[b] = n
            for pair in range(1, per_block // 2):
                extra_ref[extra] = b * 8 + pair
                extra = extra + (n > 2 * pair).astype(jnp.int32)
            total_ref[b] = part_ref[b] + pair_product(b, code, n, 0)
        return extra

    extra = lax.fori_loop(0, steps, first_pairs, jnp.int32(0))
    for at in range(BATCH):
        extra_ref[extra + at] = per_block // 2

    @pl.loop(0, (extra + BATCH - 1) // BATCH)
    def _(turn):
        products = []
        for at in range(BATCH):
            item = extra_ref[turn * BATCH + at]
            b = item // 8
            products.append((b, pair_product(b, code_ref[b], found_ref[b], lax.rem(item, 8))))
        for b, product in products:
            total_ref[b] += product

    halves = w_ref.shape[1] // 128
    stats_ref[...] = jnp.zeros_like(stats_ref)
    stats_ref[2 * halves : 2 * halves + 1, :] = jnp.full((1, 128), filled.astype(F32))

    @pl.loop(0, steps)
    def _(step):
        blocks = pl.ds(step * GROUP, GROUP)
        combined = total_ref[blocks].reshape(GROUP * rows, width).astype(BF16)
        out_ref[pl.ds(step * (GROUP * rows), GROUP * rows)] = combined
        first = jnp.dot(combined, w_ref[...], preferred_element_type=F32)
        rows_left = filled - step * (GROUP * rows)

        def add_sums(kept):
            for at, value in enumerate((kept, kept * kept)):
                line = jnp.sum(value, axis=0, keepdims=True)
                for h in range(halves):
                    spot = at * halves + h
                    stats_ref[spot : spot + 1, :] += line[:, h * 128 : (h + 1) * 128]

        @pl.when(rows_left >= GROUP * rows)
        def _():
            add_sums(first)

        @pl.when(jnp.logical_and(rows_left > 0, rows_left < GROUP * rows))
        def _():
            row_ids = lax.broadcasted_iota(jnp.int32, first.shape, 0)
            add_sums(jnp.where(row_ids < rows_left, first, 0.0))


def remote_tiles(tile_src, tile_count, node_count, recv, tiles, part, w_first):
    nb, per_block, rows = tiles.shape[:3]
    width = part.shape[2]
    lines = -(-(2 * (w_first.shape[1] // 128) + 1) // 8) * 8
    smem = pl.BlockSpec(memory_space=pltpu.SMEM)
    vmem = pl.BlockSpec(memory_space=pltpu.VMEM)
    return pl.pallas_call(
        remote_kernel,
        in_specs=[smem, smem, smem, vmem, vmem, vmem, vmem],
        out_specs=(vmem, vmem),
        out_shape=(
            jax.ShapeDtypeStruct((nb * rows, width), BF16),
            jax.ShapeDtypeStruct((lines, 128), F32),
        ),
        scratch_shapes=[
            pltpu.VMEM((nb, rows, width), F32),
            pltpu.SMEM((nb,), jnp.int32),
            pltpu.SMEM((nb,), jnp.int32),
            pltpu.SMEM((nb * per_block // 2 + BATCH,), jnp.int32),
        ],
        compiler_params=pltpu.CompilerParams(vmem_limit_bytes=REMOTE_LIMIT << 20),
    )(
        tile_src,
        tile_count,
        node_count,
        recv,
        tiles,
        part,
        w_first,
    )


def totals_kernel(n_inner, n_outer, stats_ref, out_ref, first_buf, second_buf, mid, send_sem, recv_sem):
    i, o = lax.axis_index("inner"), lax.axis_index("outer")
    inner, outer = peers_of(n_inner, n_outer)
    greet(inner + outer)
    enter(inner + outer)

    def round_of(partners, source, buf, me, base):
        copies = []
        for at, (device, _) in enumerate(partners):
            copy = pltpu.make_async_remote_copy(
                src_ref=source,
                dst_ref=buf.at[me],
                send_sem=send_sem.at[base + at],
                recv_sem=recv_sem.at[base + at],
                device_id=device,
                device_id_type=MESH,
            )
            copy.start()
            copies.append(copy)
        buf[me] = source[...]
        for copy in copies:
            copy.wait()
        return jnp.sum(buf[...], axis=0)

    mid[...] = round_of(outer, stats_ref, first_buf, o, 0)
    out_ref[...] = round_of(inner, mid, second_buf, i, len(outer))


def all_totals(mesh_sizes, stats):
    n_inner, n_outer = mesh_sizes
    partners = n_inner + n_outer - 2
    vmem = pl.BlockSpec(memory_space=pltpu.VMEM)
    return pl.pallas_call(
        functools.partial(totals_kernel, n_inner, n_outer),
        out_shape=jax.ShapeDtypeStruct(stats.shape, F32),
        in_specs=[vmem],
        out_specs=vmem,
        scratch_shapes=[
            pltpu.VMEM((n_outer,) + stats.shape, F32),
            pltpu.VMEM((n_inner,) + stats.shape, F32),
            pltpu.VMEM(stats.shape, F32),
            pltpu.SemaphoreType.DMA((partners,)),
            pltpu.SemaphoreType.DMA((partners,)),
        ],
        compiler_params=pltpu.CompilerParams(collective_id=1, has_side_effects=True, vmem_limit_bytes=2 << 20),
    )(stats)


def finish_kernel(
    node_ref,
    totals_ref,
    combined_ref,
    w1_ref,
    gamma_ref,
    beta_ref,
    w2_ref,
    bias_ref,
    out_hbm,
    stage,
    out_sem,
):
    rows = stage.shape[1]
    steps = out_hbm.shape[0] // rows
    filled = node_ref[0]
    halves = gamma_ref.shape[1] // 128

    def line(first_row):
        parts = [totals_ref[first_row + h : first_row + h + 1, :] for h in range(halves)]
        return jnp.concatenate(parts, axis=1)

    count = totals_ref[2 * halves : 2 * halves + 1, 0:1]
    mean = line(0) / count
    variance = line(halves) / count - mean * mean
    scale = gamma_ref[...] * lax.rsqrt(variance + EPSILON)

    def out_copy(step, slot):
        return pltpu.make_async_copy(
            stage.at[slot], out_hbm.at[pl.ds(step * rows, rows)], out_sem.at[slot]
        )

    @pl.loop(0, steps)
    def _(step):
        slot = lax.rem(step, 2)
        rows_left = filled - step * rows

        @pl.when(step >= 2)
        def _():
            out_copy(step - 2, slot).wait()

        def result():
            combined = combined_ref[pl.ds(step * rows, rows)]
            first = jnp.dot(combined, w1_ref[...], preferred_element_type=F32)
            normed = jnp.maximum(scale * (first - mean) + beta_ref[...], 0.0).astype(BF16)
            return jnp.dot(normed, w2_ref[...], preferred_element_type=F32) + bias_ref[...]

        @pl.when(rows_left >= rows)
        def _():
            stage[slot] = result().astype(BF16)

        @pl.when(jnp.logical_and(rows_left > 0, rows_left < rows))
        def _():
            output = result()
            row_ids = lax.broadcasted_iota(jnp.int32, output.shape, 0)
            stage[slot] = jnp.where(row_ids < rows_left, output, 0.0).astype(BF16)

        @pl.when(rows_left <= 0)
        def _():
            stage[slot] = jnp.zeros(stage.shape[1:], BF16)

        out_copy(step, slot).start()

    for step in (steps - 2, steps - 1):
        out_copy(step, step % 2).wait()


def finish(node_count, totals, combined, w_first, gamma, beta, w_second, b_second):
    nodes, width = combined.shape
    rows = nodes // 8
    smem = pl.BlockSpec(memory_space=pltpu.SMEM)
    vmem = pl.BlockSpec(memory_space=pltpu.VMEM)
    return pl.pallas_call(
        finish_kernel,
        in_specs=[smem] + [vmem] * 7,
        out_specs=pl.BlockSpec(memory_space=pltpu.HBM),
        out_shape=jax.ShapeDtypeStruct((nodes, width), BF16),
        scratch_shapes=[pltpu.VMEM((2, rows, width), BF16), pltpu.SemaphoreType.DMA((2,))],
        compiler_params=pltpu.CompilerParams(vmem_limit_bytes=FINISH_LIMIT << 20),
    )(
        node_count,
        totals,
        combined,
        w_first,
        gamma.reshape(1, -1),
        beta.reshape(1, -1),
        w_second,
        b_second.reshape(1, -1),
    )


def local(
    mesh_sizes,
    features,
    tiles,
    tile_src,
    tile_count,
    node_count,
    boundary,
    send_inner,
    count_inner,
    send_outer,
    count_outer,
    w_first,
    gamma,
    beta,
    w_second,
    b_second,
):
    nblocks, _, rows = tiles.shape[:3]
    blocks = features.reshape(nblocks, rows, features.shape[1])
    tile_src = tile_src.T
    send_outer = send_outer.transpose(0, 2, 1)
    recv, part = exchange(
        mesh_sizes, tile_src, tile_count, node_count, boundary, send_inner, send_outer, blocks, tiles
    )
    combined, stats = remote_tiles(tile_src, tile_count, node_count, recv, tiles, part, w_first)
    totals = all_totals(mesh_sizes, stats)
    return finish(node_count, totals, combined, w_first, gamma, beta, w_second, b_second)


def solution(mesh):
    both = ("inner", "outer")
    in_specs = (
        P(both, None),
        P(both, None, None, None),
        P(both, None),
        P(both),
        P(both),
        P(both, None),
        P(both, None, None),
        P(both, None),
        P(both, None, None),
        P(both, None),
        P(),
        P(),
        P(),
        P(),
        P(),
    )
    sizes = (mesh.shape["inner"], mesh.shape["outer"])
    return jax.shard_map(
        functools.partial(local, sizes),
        mesh=mesh,
        in_specs=in_specs,
        out_specs=P(both, None),
        check_vma=False,
    )
```
